32 devices in a mesh: groups: 2 (over y), adapter: 4 (over z), tensor: 2 (over x), seq: 2 (over core).
Axes of the slice: x: 2, y: 2, z: 4, core: 2. Of those that a mesh axis runs over, the one named last changes fastest.
Arguments:
- tokens: bfloat16 [2, 6144, 8192], P(None, ('groups', 'adapter', 'seq'), 'tensor'), parts along dimension 1, may hold values from -6 to 6
- token_adapter_index: int32 [2, 6144, 1], P(None, ('groups', 'adapter', 'seq')), parts along dimension 1, may hold values from 0 to 3; in each aligned block of 384 rows (0 to 383, 384 to 767, ..., all dimensions but the last counted through in order) at most 192 rows name the same one
- base_key_weight: bfloat16 [8192, 512], P(('tensor', 'seq')), may hold values from -0.0625 to 0.0625
- lowrank_down_weight: bfloat16 [4, 8192, 64], P('adapter', 'tensor'), may hold values from -0.0625 to 0.0625
- lowrank_up_weight: bfloat16 [4, 64, 512], P('adapter'), may hold values from -0.75 to 0.75
Outputs:
- keys: bfloat16 [2, 6144, 512], P(None, ('groups', 'adapter', 'seq'), 'tensor'), parts along dimension 1
The draws below stay inside these ranges and needn't reach their ends.
There are 2 independent parts, one for each index of `groups`. The reference program is written for one: setup_inputs(seed, part) draws one part's arguments, and reference() takes and returns one part's arrays. A program takes and returns all parts, laid end to end along the dimension named above; an argument that names none is the same for every part. Nothing has to cross between parts.
Inputs may be any that keep to these rules, and one draw needn't show every extreme that they name: `token_adapter_index`: in each micro-batch the 384 tokens of one device (aligned blocks along the token dimension) name one adapter at most 192 times, and in some block an adapter is named exactly 192 times; every adapter is named somewhere.
All inputs are finite; a program needn't handle non-finite values.
Results may differ from the reference program's by a relative error of at most 0.001.
Values may be sent and summed in bfloat16 or wider, within the bound.
A program may use at most 128 MiB of HBM per device.

```python
import math
import jax
import jax.numpy as jnp
import numpy as np
from jax import lax

MODEL_WIDTH = 8192
KEY_COLUMNS = 512
ADAPTER_RANK = 64
MICRO = 2
TOK_DEV = 384
ADAPTER_COUNT = 4
TOKENS = 3072
CAP = 192
N_ADAPTER = 4
N_SEQ = 2


def steps_of(key, dims, pieces, least, largest):
    def one(axis_at, shards_of):
        heights = jax.random.uniform(jax.random.fold_in(jax.random.fold_in(key, 6), axis_at), (shards_of,), jnp.float32, least / len(pieces), largest / len(pieces))
        return jnp.repeat(jnp.exp(heights), dims[axis_at] // shards_of).reshape((-1,) + (1,) * (len(dims) - axis_at - 1))

    gain = one(*pieces[0])
    for cut in pieces[1:]:
        gain = gain * one(*cut)
    return gain


def deal_out(rng, own, number, rows, count, top, most, slope):
    order = jax.random.permutation(rng, count)
    crowded, common = shares(count, rows * top, most, slope, True), shares(count, rows * top, most, slope, False)
    places = jnp.arange(count)

    def named(lengths, turn):
        used = int((lengths > 0).sum())
        fixed = max(1, used // 4)
        moved = fixed + (places - fixed + turn * (used - fixed)) % max(1, count - fixed)
        return jnp.zeros((count,), jnp.int32).at[order[jnp.where(places < fixed, places, moved)]].set(jnp.asarray(lengths, jnp.int32))

    lengths = jnp.where(number % 4 == 0, named(crowded, number // 4), named(common, number - number // 4 - 1))
    mixed = jax.random.permutation(jax.random.fold_in(own, 3), count)
    donor, taker = mixed[0:count // 2 * 2:2], mixed[1:count // 2 * 2:2]
    slack = jnp.minimum(lengths[donor] - 1, most - lengths[taker]) // 2
    slack = jnp.where((donor == order[0]) | (taker == order[0]) | (lengths[taker] == 0), 0, jnp.maximum(slack, 0))
    moved = jax.random.randint(jax.random.fold_in(own, 4), (count // 2,), 0, 1 << 20) % (slack + 1)
    lengths = lengths.at[donor].add(-moved).at[taker].add(moved)
    items = jnp.searchsorted(jnp.cumsum(lengths), jnp.arange(rows * top), side="right").astype(jnp.int32)
    grid = items.reshape(top, rows).T
    grid = grid[jax.random.permutation(jax.random.fold_in(own, 1), rows)]
    turn = jax.random.randint(jax.random.fold_in(own, 2), (rows, 1), 0, top)
    return jnp.take_along_axis(grid, (jnp.arange(top)[None, :] + turn) % top, axis=1)


def shares(amount, total, bound, skew, full):
    weights = [(1 << 20) // math.isqrt(grade ** skew) + 1 for grade in range(1, amount + 1)]
    largest = bound if full else min(bound, max(-(-total // amount), total * weights[0] // sum(weights)))
    least = 1 if total - largest >= amount - 1 else 0
    counts, spare = [largest] + [least] * (amount - 1), total - largest - least * (amount - 1)
    while spare > 0:
        movable = [i for i in range(1, amount) if counts[i] < largest] or [i for i in range(1, amount) if counts[i] < bound]
        mass, remaining = sum([weights[i] for i in movable]), spare
        for i in movable:
            more = min(bound - counts[i], max(1, remaining * weights[i] // mass), spare)
            counts[i] = counts[i] + more
            spare = spare - more
    return np.array(counts)


def centred(stream_key, dims, scale, reach, pieces=(), kind=jnp.bfloat16):
    loudness = steps_of(stream_key, dims, pieces, -0.22, 0.18) if pieces else 1.0
    entries = jax.random.normal(stream_key, dims, jnp.float32) * scale * loudness
    return jnp.minimum(jnp.maximum(entries, -reach), reach).astype(kind)


def setup_inputs(seed: int = 0, part: int = 0) -> dict:
    streams_of = jax.random.split(jax.random.key(seed), 6)
    part_splits = jax.random.split(jax.random.fold_in(streams_of[5], part), 6)
    tokens = centred(part_splits[0], (MICRO, TOKENS, MODEL_WIDTH), 1.0, 6.0, ((1, 8), (2, 2)))
    token_adapter_index_keys = jax.random.split(jax.random.fold_in(part_splits[1], 1), MICRO * TOKENS // TOK_DEV)
    token_adapter_index_turns = jax.random.permutation(jax.random.fold_in(part_splits[1], 3), MICRO * TOKENS // TOK_DEV)
    token_adapter_index = jax.vmap(lambda own, number: deal_out(jax.random.fold_in(part_splits[1], 2), own, number, TOK_DEV, ADAPTER_COUNT, 1, CAP, 2))(token_adapter_index_keys, token_adapter_index_turns).reshape((MICRO, TOKENS, 1))
    base_key_weight = centred(streams_of[2], (MODEL_WIDTH, KEY_COLUMNS), MODEL_WIDTH ** -0.5, 0.0625, ((0, 4),))
    lowrank_down_weight = centred(streams_of[3], (ADAPTER_COUNT, MODEL_WIDTH, ADAPTER_RANK), MODEL_WIDTH ** -0.5, 0.0625, ((0, 4), (1, 2)))
    lowrank_up_weight = centred(streams_of[4], (ADAPTER_COUNT, ADAPTER_RANK, KEY_COLUMNS), ADAPTER_RANK ** -0.5, 0.75, ((0, 4),))
    return {"tokens": tokens, "token_adapter_index": token_adapter_index, "base_key_weight": base_key_weight, "lowrank_down_weight": lowrank_down_weight, "lowrank_up_weight": lowrank_up_weight}


def reference(tokens, token_adapter_index, base_key_weight, lowrank_down_weight, lowrank_up_weight):
    chosen_all = token_adapter_index[:, :, 0]
    room = N_ADAPTER * N_SEQ * CAP
    results = []
    for batch_index in range(MICRO):
        features = tokens[batch_index]
        chosen = chosen_all[batch_index]
        onehot = (chosen[:, None] == jnp.arange(ADAPTER_COUNT, dtype=jnp.int32)[None, :]).astype(jnp.int32)
        before = jnp.cumsum(onehot, axis=0) - onehot
        position = jnp.sum(before * onehot, axis=1).astype(jnp.int32)
        slots = (chosen * room + position).astype(jnp.int32)
        filler = jnp.full((ADAPTER_COUNT * room,), TOKENS, jnp.int32)
        source_tokens = filler.at[slots].set(jnp.arange(TOKENS, dtype=jnp.int32)).reshape(ADAPTER_COUNT, room)
        padded = jnp.concatenate([features, jnp.zeros((1, MODEL_WIDTH), features.dtype)], axis=0)

        def single_adapter(packed):
            rows_index, down, upper = packed
            block = padded[rows_index]
            reduced = jnp.dot(block, down, preferred_element_type=jnp.float32)
            return jnp.dot(reduced, upper.astype(jnp.float32), precision=lax.Precision.HIGHEST)

        adapter_output = lax.map(single_adapter, (source_tokens, lowrank_down_weight, lowrank_up_weight))
        adapter_output = adapter_output.reshape(ADAPTER_COUNT * room, KEY_COLUMNS)[slots]
        base_part = jnp.dot(features, base_key_weight, preferred_element_type=jnp.float32)
        results.append((base_part + adapter_output).astype(jnp.bfloat16))
    return jnp.stack(results, axis=0)
```

```python
import functools

import jax
import jax.numpy as jnp
from jax import lax
from jax.experimental import pallas as pl
from jax.experimental.pallas import tpu as pltpu
from jax.sharding import PartitionSpec as P

F32 = jnp.float32
BF16 = jnp.bfloat16
MESH = pl.DeviceIdType.MESH


def remote(src, dst, send, recv, device):
    return pltpu.make_async_remote_copy(
        src_ref=src, dst_ref=dst, send_sem=send, recv_sem=recv, device_id=device, device_id_type=MESH
    )


def kernel(
    sizes, chunk,
    idx_ref, x_hbm, w_hbm, d_hbm, u_hbm, o_hbm,
    index_v, x_v, w_v, d_v, u_v, base_send, base_recv, base_own, z_own, z_recv, o_v,
    x_sem, load_sem, out_sem, w_sem, pz_sem, py_sem, pc_sem, uz_sem, uy_sem, uc_sem, base_sem, z_sem,
):
    n_g, n_a, n_t, n_s = sizes
    g, a, t, s = [lax.axis_index(name) for name in ("groups", "adapter", "tensor", "seq")]
    rows, width = x_v.shape
    rank = d_hbm.shape[1]
    n_q = n_g * n_s
    part = rank // n_q
    cols = o_v.shape[1]
    steps = rows // chunk
    w_rows = w_hbm.shape[0]

    def load_x(i):
        at = pl.ds(pl.multiple_of(i * chunk, chunk), chunk)
        return pltpu.make_async_copy(x_hbm.at[at], x_v.at[at], x_sem.at[i])

    own_w = pl.ds(pl.multiple_of(s * w_rows, w_rows), w_rows)
    own_cols = pl.ds(pl.multiple_of(t * cols, cols), cols)
    own_rank = pl.ds(pl.multiple_of(a * rank, rank), rank)
    load_d = pltpu.make_async_copy(d_hbm.at[0], d_v.at[own_rank], load_sem.at[0])
    load_u = pltpu.make_async_copy(u_hbm.at[0, :, own_cols], u_v.at[own_rank], load_sem.at[1])
    load_w = pltpu.make_async_copy(w_hbm, w_v.at[own_w], load_sem.at[2])
    load_d.start()
    load_u.start()
    load_w.start()
    for i in range(steps):
        load_x(i).start()

    barrier = pltpu.get_barrier_semaphore()
    peers = [("groups", g, n_g), ("adapter", a, n_a), ("tensor", t, n_t), ("seq", s, n_s)]
    for name, at, size in peers:
        for j in range(1, size):
            pl.semaphore_signal(
                barrier, inc=1, device_id={name: lax.rem(at + j, size)}, device_id_type=MESH
            )

    for i in range(rows // 128):
        line = jnp.broadcast_to(idx_ref[:, i * 128 : (i + 1) * 128], (128, 128))
        index_v[i * 128 : (i + 1) * 128] = line.T

    load_d.wait()
    load_u.wait()
    pl.semaphore_wait(barrier, sum(size - 1 for _, _, size in peers))

    def send_w(j):
        return remote(
            w_hbm, w_v.at[own_w], w_sem.at[0, j], w_sem.at[1, j], {"seq": lax.rem(s + j, n_s)}
        )

    for j in range(1, n_s):
        send_w(j).start()

    def parts(b, q, sems_p, sems_u, k, device):
        at = pl.ds(pl.multiple_of(b * rank + q * part, part), part)
        p_at, u_at = d_v.at[at], u_v.at[at]
        return (
            remote(p_at, p_at, sems_p.at[0, k], sems_p.at[1, k], device),
            remote(u_at, u_at, sems_u.at[0, k], sems_u.at[1, k], device),
        )

    def along_a(d, source):
        return parts(source, g * n_s + s, pz_sem, uz_sem, d, {"adapter": lax.rem(a + d, n_a)})

    def along_g(d, j, owner):
        b = lax.rem(a + n_a - d, n_a)
        return parts(b, owner * n_s + s, py_sem, uy_sem, d * n_g + j, {"groups": lax.rem(g + j, n_g)})

    def along_s(d, e, j, owner):
        b = lax.rem(a + n_a - d, n_a)
        q = lax.rem(g + n_g - e, n_g) * n_s + owner
        return parts(b, q, pc_sem, uc_sem, (d * n_g + e) * n_s + j, {"seq": lax.rem(s + j, n_s)})

    for d in range(1, n_a):
        for copy in along_a(d, a):
            copy.start()

    load_w.wait()
    for j in range(1, n_s):
        sent = send_w(j)
        other = lax.rem(s + n_s - j, n_s)
        remote(
            w_hbm, w_v.at[pl.ds(pl.multiple_of(other * w_rows, w_rows), w_rows)],
            w_sem.at[0, j], w_sem.at[1, j], {"seq": lax.rem(s + j, n_s)},
        ).wait_recv()
        sent.wait_send()

    def at_rows(i, size=chunk):
        return pl.ds(pl.multiple_of(i * size, size), size)

    def send_base(j, i):
        return remote(
            base_send.at[j - 1, at_rows(i)], base_recv.at[j - 1, at_rows(i)],
            base_sem.at[0, (j - 1) * steps + i], base_sem.at[1, (j - 1) * steps + i],
            {"tensor": lax.rem(t + j, n_t)},
        )

    for j in range(1, n_t):
        their = pl.ds(pl.multiple_of(lax.rem(t + j, n_t) * cols, cols), cols)

        def other_columns(i, _):
            if j == 1:
                load_x(i).wait()
            base_send[j - 1, at_rows(i)] = jnp.dot(
                x_v[at_rows(i)], w_v[:, their], preferred_element_type=F32
            )
            send_base(j, i).start()
            return 0

        lax.fori_loop(0, steps, other_columns, 0)

    for d in range(1, n_a):
        for copy in along_a(d, lax.rem(a + n_a - d, n_a)):
            copy.wait_recv()
        for j in range(1, n_g):
            for copy in along_g(d, j, g):
                copy.start()
        for j in range(1, n_s):
            for copy in along_s(d, 0, j, s):
                copy.start()

    def own_columns(i, _):
        base_own[at_rows(i)] = jnp.dot(
            x_v[at_rows(i)], w_v[:, own_cols], preferred_element_type=F32
        )
        return 0

    lax.fori_loop(0, steps, own_columns, 0)

    for d in range(1, n_a):
        for j in range(1, n_g):
            for copy in along_g(d, j, lax.rem(g + n_g - j, n_g)):
                copy.wait_recv()
            for k in range(1, n_s):
                for copy in along_s(d, j, k, s):
                    copy.start()
    for d in range(1, n_a):
        for e in range(n_g):
            for k in range(1, n_s):
                for copy in along_s(d, e, k, lax.rem(s + n_s - k, n_s)):
                    copy.wait_recv()

    short = chunk // 2

    def send_z(j, i):
        return remote(
            z_own.at[at_rows(i, short)], z_recv.at[j - 1, at_rows(i, short)],
            z_sem.at[0, (j - 1) * steps + i], z_sem.at[1, (j - 1) * steps + i],
            {"tensor": lax.rem(t + j, n_t)},
        )

    def low_rank(i, _):
        index = index_v[at_rows(i)]
        partial = lax.dot_general(
            x_v[at_rows(i)], d_v[...], (((1,), (1,)), ((), ())), preferred_element_type=F32
        )
        lane = lax.broadcasted_iota(jnp.int32, (chunk, 2 * rank), 1)
        is_right = (lane >= rank).astype(jnp.int32)
        total = jnp.zeros((chunk, 2 * rank), F32)
        for pair in range(n_a // 2):
            at = slice(2 * rank * pair, 2 * rank * (pair + 1))
            total += jnp.where(index == 2 * pair + is_right, partial[:, at], 0.0)
        total = total + pltpu.roll(total, rank, 1)
        z_own[at_rows(i, short)] = jnp.where(lane[:short] < rank, total[:short], total[short:])
        for j in range(1, n_t):
            send_z(j, i).start()
        return 0

    lax.fori_loop(0, steps, low_rank, 0)

    def store_out(i):
        return pltpu.make_async_copy(o_v.at[at_rows(i)], o_hbm.at[at_rows(i)], out_sem.at[i])

    def finish(i, _):
        z = z_own[at_rows(i, short)]
        total = base_own[at_rows(i)]
        for j in range(1, n_t):
            send_base(j, i).wait_recv()
            total = total + base_recv[j - 1, at_rows(i)]
        for j in range(1, n_t):
            send_z(j, i).wait_recv()
            z = z + z_recv[j - 1, at_rows(i, short)]
        turned = pltpu.roll(z, rank, 1)
        left = lax.broadcasted_iota(jnp.int32, (short, 2 * rank), 1) < rank
        both = jnp.concatenate([jnp.where(left, z, turned), jnp.where(left, turned, z)], axis=0)
        lane = lax.broadcasted_iota(jnp.int32, (chunk, 2 * rank), 1)
        is_right = (lane >= rank).astype(jnp.int32)
        index = index_v[at_rows(i)]
        spread = jnp.concatenate(
            [jnp.where(index == 2 * pair + is_right, both, 0.0) for pair in range(n_a // 2)], axis=1
        )
        high = spread.astype(BF16)
        low = (spread - high.astype(F32)).astype(BF16)
        total = total + jnp.dot(high, u_v[...], preferred_element_type=F32)
        total = total + jnp.dot(low, u_v[...], preferred_element_type=F32)
        o_v[at_rows(i)] = total.astype(BF16)
        store_out(i).start()
        return 0

    lax.fori_loop(0, steps, finish, 0)

    for d in range(1, n_a):
        for copy in along_a(d, a):
            copy.wait_send()
        for j in range(1, n_g):
            for copy in along_g(d, j, g):
                copy.wait_send()
        for e in range(n_g):
            for k in range(1, n_s):
                for copy in along_s(d, e, k, s):
                    copy.wait_send()
    for i in range(steps):
        for j in range(1, n_t):
            send_base(j, i).wait_send()
            send_z(j, i).wait_send()
        store_out(i).wait()


def local(sizes, tokens, token_adapter_index, base_key_weight, lowrank_down_weight, lowrank_up_weight):
    n_g, n_a, n_t, n_s = sizes
    micro, tok_rows, width = tokens.shape
    rows = micro * tok_rows
    key_cols = base_key_weight.shape[1]
    cols = key_cols // n_t
    rank = lowrank_down_weight.shape[2]
    chunk = rows // 4
    steps = rows // chunk
    any_space = pl.BlockSpec(memory_space=pl.ANY)
    dma = pltpu.SemaphoreType.DMA
    out = pl.pallas_call(
        functools.partial(kernel, sizes, chunk),
        out_shape=jax.ShapeDtypeStruct((rows, cols), BF16),
        in_specs=[pl.BlockSpec(memory_space=pltpu.VMEM)] + [any_space] * 4,
        out_specs=any_space,
        scratch_shapes=[
            pltpu.VMEM((rows, 2 * rank), jnp.int32),
            pltpu.VMEM((rows, width), BF16),
            pltpu.VMEM((width, key_cols), BF16),
            pltpu.VMEM((n_a * rank, width), BF16),
            pltpu.VMEM((n_a * rank, cols), BF16),
            pltpu.VMEM((n_t - 1, rows, cols), F32),
            pltpu.VMEM((n_t - 1, rows, cols), F32),
            pltpu.VMEM((rows, cols), F32),
            pltpu.VMEM((rows // 2, 2 * rank), F32),
            pltpu.VMEM((n_t - 1, rows // 2, 2 * rank), F32),
            pltpu.VMEM((rows, cols), BF16),
            dma((steps,)),
            dma((3,)),
            dma((steps,)),
            dma((2, n_s)),
            dma((2, n_a)),
            dma((2, n_a * n_g)),
            dma((2, n_a * n_g * n_s)),
            dma((2, n_a)),
            dma((2, n_a * n_g)),
            dma((2, n_a * n_g * n_s)),
            dma((2, (n_t - 1) * steps)),
            dma((2, (n_t - 1) * steps)),
        ],
        compiler_params=pltpu.CompilerParams(
            collective_id=0, has_side_effects=True, vmem_limit_bytes=56 * 1024 * 1024
        ),
    )(
        token_adapter_index.reshape(1, rows),
        tokens.reshape(rows, width),
        base_key_weight,
        jnp.swapaxes(lowrank_down_weight, 1, 2),
        lowrank_up_weight,
    )
    return out.reshape(micro, tok_rows, cols)


def solution(mesh):
    sizes = tuple(mesh.shape[name] for name in ("groups", "adapter", "tensor", "seq"))
    placed = (
        P(None, ("groups", "adapter", "seq"), "tensor"),
        P(None, ("groups", "adapter", "seq"), None),
        P(("tensor", "seq"), None),
        P("adapter", "tensor", None),
        P("adapter", None, None),
    )
    return jax.shard_map(
        functools.partial(local, sizes),
        mesh=mesh,
        in_specs=placed,
        out_specs=P(None, ("groups", "adapter", "seq"), "tensor"),
        check_vma=False,
    )
```

```python
import functools

import jax
import jax.numpy as jnp
from jax import lax
from jax.experimental import pallas as pl
from jax.experimental.pallas import tpu as pltpu
from jax.sharding import PartitionSpec as P

F32 = jnp.float32
BF16 = jnp.bfloat16
MESH = pl.DeviceIdType.MESH


def remote(src, dst, send, recv, device):
    return pltpu.make_async_remote_copy(
        src_ref=src, dst_ref=dst, send_sem=send, recv_sem=recv, device_id=device, device_id_type=MESH
    )


def coded(value):
    top = jnp.maximum(jnp.max(jnp.abs(value), axis=0, keepdims=True), 1e-30)
    return jnp.round(value * (32767.0 / top)).astype(jnp.int32).astype(jnp.int16), top * (1.0 / 32767.0)


def decoded(code, step):
    return code.astype(jnp.int32).astype(F32) * step


def kernel(
    sizes, chunk,
    idx_ref, x_hbm, w_hbm, d_hbm, u_hbm, o_hbm,
    index_v, x_v, w_v, d_v, turned_v, reduced_v, u_v,
    base_part, base_send, base_recv, step_send, step_recv, base_own, z_own, z_recv, o_v,
    x_sem, load_sem, out_sem, w_sem, pz_sem, py_sem, pc_sem, uz_sem, uy_sem, uc_sem, base_sem, step_sem, z_sem,
):
    n_g, n_a, n_t, n_s = sizes
    g, a, t, s = [lax.axis_index(name) for name in ("groups", "adapter", "tensor", "seq")]
    rows, width = x_v.shape
    rank = d_hbm.shape[1]
    n_q = n_g * n_s
    part, span = rank // n_q, width // n_q
    cols = o_v.shape[1]
    steps = rows // chunk
    w_rows = w_hbm.shape[0]

    def at_rows(i, size=chunk):
        return pl.ds(pl.multiple_of(i * size, size), size)

    def load_x(i):
        return pltpu.make_async_copy(x_hbm.at[at_rows(i)], x_v.at[at_rows(i)], x_sem.at[i])

    own_w = at_rows(s, w_rows)
    own_cols = at_rows(t, cols)
    own_rank = at_rows(a, rank)
    load_d = pltpu.make_async_copy(d_hbm.at[0], d_v.at[own_rank], load_sem.at[0])
    load_u = pltpu.make_async_copy(u_hbm.at[0, :, own_cols], u_v.at[own_rank], load_sem.at[1])
    load_w = pltpu.make_async_copy(w_hbm, w_v.at[own_w], load_sem.at[2])
    load_d.start()
    load_u.start()
    load_w.start()
    for i in range(steps):
        load_x(i).start()

    barrier = pltpu.get_barrier_semaphore()
    peers = [("groups", g, n_g), ("adapter", a, n_a), ("tensor", t, n_t), ("seq", s, n_s)]
    for name, at, size in peers:
        for j in range(1, size):
            pl.semaphore_signal(
                barrier, inc=1, device_id={name: lax.rem(at + j, size)}, device_id_type=MESH
            )

    for i in range(rows // 128):
        line = jnp.broadcast_to(idx_ref[:, i * 128 : (i + 1) * 128], (128, 128))
        index_v[i * 128 : (i + 1) * 128] = line.T

    load_d.wait()
    load_u.wait()
    pl.semaphore_wait(barrier, sum(size - 1 for _, _, size in peers))

    def parts(b, q, sems_p, sems_u, k, device):
        p_at = d_v.at[at_rows(b, rank), at_rows(q, span)]
        u_at = u_v.at[pl.ds(pl.multiple_of(b * rank + q * part, part), part)]
        return (
            remote(p_at, p_at, sems_p.at[0, k], sems_p.at[1, k], device),
            remote(u_at, u_at, sems_u.at[0, k], sems_u.at[1, k], device),
        )

    def along_a(d, source):
        return parts(source, g * n_s + s, pz_sem, uz_sem, d, {"adapter": lax.rem(a + d, n_a)})

    def along_g(d, j, owner):
        b = lax.rem(a + n_a - d, n_a)
        return parts(b, owner * n_s + s, py_sem, uy_sem, d * n_g + j, {"groups": lax.rem(g + j, n_g)})

    def along_s(d, e, j, owner):
        b = lax.rem(a + n_a - d, n_a)
        q = lax.rem(g + n_g - e, n_g) * n_s + owner
        return parts(b, q, pc_sem, uc_sem, (d * n_g + e) * n_s + j, {"seq": lax.rem(s + j, n_s)})

    near_first = sorted(range(1, n_a), key=lambda d: (min(d, n_a - d), d))
    for d in near_first:
        for copy in along_a(d, a):
            copy.start()

    def send_w(j, k, owner):
        at = at_rows(lax.rem(t + k, n_t), cols)
        return remote(
            w_hbm.at[:, at], w_v.at[at_rows(owner, w_rows), at],
            w_sem.at[0, j * n_t + k], w_sem.at[1, j * n_t + k], {"seq": lax.rem(s + j, n_s)},
        )

    order = list(range(1, n_t)) + [0]
    for k in order:
        for j in range(1, n_s):
            send_w(j, k, s).start()

    load_w.wait()

    def own_rows(i, _):
        load_x(i).wait()
        for k in range(n_t):
            base_part[k, at_rows(i)] = jnp.dot(
                x_v[at_rows(i), own_w], w_v[own_w, at_rows(lax.rem(t + k, n_t), cols)],
                preferred_element_type=F32,
            )
        return 0

    lax.fori_loop(0, steps, own_rows, 0)

    def other_rows(i, k):
        total = base_part[k, at_rows(i)]
        for j in range(1, n_s):
            at = at_rows(lax.rem(s + j, n_s), w_rows)
            total = total + jnp.dot(
                x_v[at_rows(i), at], w_v[at, at_rows(lax.rem(t + k, n_t), cols)],
                preferred_element_type=F32,
            )
        return total

    def send_base(j, i):
        k = (j - 1) * steps + i
        device = {"tensor": lax.rem(t + j, n_t)}
        return (
            remote(
                base_send.at[j - 1, at_rows(i)], base_recv.at[j - 1, at_rows(i)],
                base_sem.at[0, k], base_sem.at[1, k], device,
            ),
            remote(
                step_send.at[k], step_recv.at[k], step_sem.at[0, k], step_sem.at[1, k], device
            ),
        )

    for k in range(1, n_t):
        for j in range(1, n_s):
            send_w(j, k, lax.rem(s + n_s - j, n_s)).wait_recv()

        def other_columns(i, _):
            code, step = coded(other_rows(i, k))
            base_send[k - 1, at_rows(i)] = code
            step_send[(k - 1) * steps + i] = jnp.broadcast_to(step, step_send.shape[1:])
            for copy in send_base(k, i):
                copy.start()
            return 0

        lax.fori_loop(0, steps, other_columns, 0)

    def pass_on(d):
        for copy in along_a(d, lax.rem(a + n_a - d, n_a)):
            copy.wait_recv()
        for j in range(1, n_g):
            for copy in along_g(d, j, g):
                copy.start()
        for j in range(1, n_s):
            for copy in along_s(d, 0, j, s):
                copy.start()

    early = len(near_first) * 2 // 3
    for d in near_first[:early]:
        pass_on(d)

    for j in range(1, n_s):
        send_w(j, 0, lax.rem(s + n_s - j, n_s)).wait_recv()

    def own_columns(i, _):
        base_own[at_rows(i)] = other_rows(i, 0)
        return 0

    lax.fori_loop(0, steps, own_columns, 0)

    for d in near_first[early:]:
        pass_on(d)

    def reduce_part(q, fresh):
        at = at_rows(q, span)
        turned_v[...] = d_v[:, at].T

        def some(i, _):
            more = jnp.dot(x_v[at_rows(i), at], turned_v[...], preferred_element_type=F32)
            reduced_v[at_rows(i)] = more if fresh else reduced_v[at_rows(i)] + more
            return 0

        lax.fori_loop(0, steps, some, 0)

    reduce_part(g * n_s + s, True)
    for d in near_first:
        for j in range(1, n_g):
            for copy in along_g(d, j, lax.rem(g + n_g - j, n_g)):
                copy.wait_recv()
            for k in range(1, n_s):
                for copy in along_s(d, j, k, s):
                    copy.start()
    for e in range(n_g):
        at_g = lax.rem(g + n_g - e, n_g) * n_s
        if e:
            reduce_part(at_g + s, False)
        for k in range(1, n_s):
            owner = lax.rem(s + n_s - k, n_s)
            for d in near_first:
                for copy in along_s(d, e, k, owner):
                    copy.wait_recv()
            reduce_part(at_g + owner, False)

    short = chunk // 2

    def send_z(j, i):
        return remote(
            z_own.at[at_rows(i, short)], z_recv.at[j - 1, at_rows(i, short)],
            z_sem.at[0, (j - 1) * steps + i], z_sem.at[1, (j - 1) * steps + i],
            {"tensor": lax.rem(t + j, n_t)},
        )

    def low_rank(i, _):
        index = index_v[at_rows(i)]
        partial = reduced_v[at_rows(i)]
        lane = lax.broadcasted_iota(jnp.int32, (chunk, 2 * rank), 1)
        is_right = (lane >= rank).astype(jnp.int32)
        total = jnp.zeros((chunk, 2 * rank), F32)
        for pair in range(n_a // 2):
            at = slice(2 * rank * pair, 2 * rank * (pair + 1))
            total += jnp.where(index == 2 * pair + is_right, partial[:, at], 0.0)
        total = total + pltpu.roll(total, rank, 1)
        z_own[at_rows(i, short)] = jnp.where(lane[:short] < rank, total[:short], total[short:])
        for j in range(1, n_t):
            send_z(j, i).start()
        return 0

    lax.fori_loop(0, steps, low_rank, 0)

    def store_out(i):
        return pltpu.make_async_copy(o_v.at[at_rows(i)], o_hbm.at[at_rows(i)], out_sem.at[i])

    def finish(i, _):
        z = z_own[at_rows(i, short)]
        total = base_own[at_rows(i)]
        for j in range(1, n_t):
            for copy in send_base(j, i):
                copy.wait_recv()
            total = total + decoded(
                base_recv[j - 1, at_rows(i)], step_recv[(j - 1) * steps + i][:1]
            )
        for j in range(1, n_t):
            send_z(j, i).wait_recv()
            z = z + z_recv[j - 1, at_rows(i, short)]
        turned = pltpu.roll(z, rank, 1)
        left = lax.broadcasted_iota(jnp.int32, (short, 2 * rank), 1) < rank
        both = jnp.concatenate([jnp.where(left, z, turned), jnp.where(left, turned, z)], axis=0)
        lane = lax.broadcasted_iota(jnp.int32, (chunk, 2 * rank), 1)
        is_right = (lane >= rank).astype(jnp.int32)
        index = index_v[at_rows(i)]
        spread = jnp.concatenate(
            [jnp.where(index == 2 * pair + is_right, both, 0.0) for pair in range(n_a // 2)], axis=1
        )
        high = spread.astype(BF16)
        low = (spread - high.astype(F32)).astype(BF16)
        total = total + jnp.dot(high, u_v[...], preferred_element_type=F32)
        total = total + jnp.dot(low, u_v[...], preferred_element_type=F32)
        o_v[at_rows(i)] = total.astype(BF16)
        store_out(i).start()
        return 0

    lax.fori_loop(0, steps, finish, 0)

    for k in order:
        for j in range(1, n_s):
            send_w(j, k, s).wait_send()
    for d in range(1, n_a):
        for copy in along_a(d, a):
            copy.wait_send()
        for j in range(1, n_g):
            for copy in along_g(d, j, g):
                copy.wait_send()
        for e in range(n_g):
            for k in range(1, n_s):
                for copy in along_s(d, e, k, s):
                    copy.wait_send()
    for i in range(steps):
        for j in range(1, n_t):
            for copy in send_base(j, i):
                copy.wait_send()
            send_z(j, i).wait_send()
        store_out(i).wait()


def local(sizes, tokens, token_adapter_index, base_key_weight, lowrank_down_weight, lowrank_up_weight):
    n_g, n_a, n_t, n_s = sizes
    micro, tok_rows, width = tokens.shape
    rows = micro * tok_rows
    key_cols = base_key_weight.shape[1]
    cols = key_cols // n_t
    rank = lowrank_down_weight.shape[2]
    chunk = rows // 4
    steps = rows // chunk
    any_space = pl.BlockSpec(memory_space=pl.ANY)
    dma = pltpu.SemaphoreType.DMA
    out = pl.pallas_call(
        functools.partial(kernel, sizes, chunk),
        out_shape=jax.ShapeDtypeStruct((rows, cols), BF16),
        in_specs=[pl.BlockSpec(memory_space=pltpu.VMEM)] + [any_space] * 4,
        out_specs=any_space,
        scratch_shapes=[
            pltpu.VMEM((rows, 2 * rank), jnp.int32),
            pltpu.VMEM((rows, width), BF16),
            pltpu.VMEM((width, key_cols), BF16),
            pltpu.VMEM((n_a * rank, width), BF16),
            pltpu.VMEM((width // (n_g * n_s), n_a * rank), BF16),
            pltpu.VMEM((rows, n_a * rank), F32),
            pltpu.VMEM((n_a * rank, cols), BF16),
            pltpu.VMEM((n_t, rows, cols), F32),
            pltpu.VMEM((n_t - 1, rows, cols), jnp.int16),
            pltpu.VMEM((n_t - 1, rows, cols), jnp.int16),
            pltpu.VMEM(((n_t - 1) * steps, 8, cols), F32),
            pltpu.VMEM(((n_t - 1) * steps, 8, cols), F32),
            pltpu.VMEM((rows, cols), F32),
            pltpu.VMEM((rows // 2, 2 * rank), F32),
            pltpu.VMEM((n_t - 1, rows // 2, 2 * rank), F32),
            pltpu.VMEM((rows, cols), BF16),
            dma((steps,)),
            dma((3,)),
            dma((steps,)),
            dma((2, n_s * n_t)),
            dma((2, n_a)),
            dma((2, n_a * n_g)),
            dma((2, n_a * n_g * n_s)),
            dma((2, n_a)),
            dma((2, n_a * n_g)),
            dma((2, n_a * n_g * n_s)),
            dma((2, (n_t - 1) * steps)),
            dma((2, (n_t - 1) * steps)),
            dma((2, (n_t - 1) * steps)),
        ],
        compiler_params=pltpu.CompilerParams(
            collective_id=0, has_side_effects=True, vmem_limit_bytes=56 * 1024 * 1024
        ),
    )(
        token_adapter_index.reshape(1, rows),
        tokens.reshape(rows, width),
        base_key_weight,
        jnp.swapaxes(lowrank_down_weight, 1, 2),
        lowrank_up_weight,
    )
    return out.reshape(micro, tok_rows, cols)


def solution(mesh):
    sizes = tuple(mesh.shape[name] for name in ("groups", "adapter", "tensor", "seq"))
    placed = (
        P(None, ("groups", "adapter", "seq"), "tensor"),
        P(None, ("groups", "adapter", "seq"), None),
        P(("tensor", "seq"), None),
        P("adapter", "tensor", None),
        P("adapter", None, None),
    )
    return jax.shard_map(
        functools.partial(local, sizes),
        mesh=mesh,
        in_specs=placed,
        out_specs=P(None, ("groups", "adapter", "seq"), "tensor"),
        check_vma=False,
    )
```

```python
import functools

import jax
import jax.numpy as jnp
from jax import lax
from jax.experimental import pallas as pl
from jax.experimental.pallas import tpu as pltpu
from jax.sharding import PartitionSpec as P

F32 = jnp.float32
BF16 = jnp.bfloat16
MESH = pl.DeviceIdType.MESH


def remote(src, dst, send, recv, device):
    return pltpu.make_async_remote_copy(
        src_ref=src, dst_ref=dst, send_sem=send, recv_sem=recv, device_id=device, device_id_type=MESH
    )


def coded(value):
    top = jnp.maximum(jnp.max(jnp.abs(value), axis=0, keepdims=True), 1e-30)
    return jnp.round(value * (32767.0 / top)).astype(jnp.int32).astype(jnp.int16), top * (1.0 / 32767.0)


def decoded(code, step):
    return code.astype(jnp.int32).astype(F32) * step


def kernel(
    sizes, chunk,
    idx_ref, x_hbm, w_hbm, d_hbm, u_hbm, o_hbm,
    index_v, x_v, w_v, d_v, turned_v, reduced_v, u_v,
    base_part, base_send, base_recv, step_send, step_recv, base_own, z_own, z_send, z_recv, z_step_send, z_step_recv, o_v,
    x_sem, load_sem, out_sem, w_sem, pz_sem, py_sem, pc_sem, uz_sem, base_sem, step_sem, z_sem, z_step_sem,
):
    n_g, n_a, n_t, n_s = sizes
    g, a, t, s = [lax.axis_index(name) for name in ("groups", "adapter", "tensor", "seq")]
    rows, width = x_v.shape
    rank = d_hbm.shape[1]
    n_q = n_g * n_s
    span = width // n_q
    cols = o_v.shape[1]
    steps = rows // chunk
    w_rows = w_hbm.shape[0]

    def at_rows(i, size=chunk):
        return pl.ds(pl.multiple_of(i * size, size), size)

    def load_x(i):
        return pltpu.make_async_copy(x_hbm.at[at_rows(i)], x_v.at[at_rows(i)], x_sem.at[i])

    own_w = at_rows(s, w_rows)
    own_cols = at_rows(t, cols)
    own_rank = at_rows(a, rank)
    load_d = pltpu.make_async_copy(d_hbm.at[0], d_v.at[own_rank], load_sem.at[0])
    load_u = pltpu.make_async_copy(u_hbm.at[0, :, own_cols], u_v.at[own_rank], load_sem.at[1])
    load_w = pltpu.make_async_copy(w_hbm, w_v.at[own_w], load_sem.at[2])
    load_d.start()
    load_u.start()
    load_w.start()

    barrier = pltpu.get_barrier_semaphore()
    peers = [("groups", g, n_g), ("adapter", a, n_a), ("tensor", t, n_t), ("seq", s, n_s)]
    for name, at, size in peers:
        for j in range(1, size):
            pl.semaphore_signal(
                barrier, inc=1, device_id={name: lax.rem(at + j, size)}, device_id_type=MESH
            )

    for i in range(rows // 128):
        line = jnp.broadcast_to(idx_ref[:, i * 128 : (i + 1) * 128], (128, 128))
        index_v[i * 128 : (i + 1) * 128] = line.T

    load_d.wait()
    load_u.wait()
    pl.semaphore_wait(barrier, sum(size - 1 for _, _, size in peers))

    def parts(b, q, sems_p, k, device):
        p_at = d_v.at[at_rows(b, rank), at_rows(q, span)]
        return (remote(p_at, p_at, sems_p.at[0, k], sems_p.at[1, k], device),)

    def send_u(d, source):
        at = u_v.at[at_rows(source, rank)]
        return remote(at, at, uz_sem.at[0, d], uz_sem.at[1, d], {"adapter": lax.rem(a + d, n_a)})

    def along_a(d, source):
        return parts(source, g * n_s + s, pz_sem, d, {"adapter": lax.rem(a + d, n_a)})

    def along_g(d, j, owner):
        b = lax.rem(a + n_a - d, n_a)
        return parts(b, owner * n_s + s, py_sem, d * n_g + j, {"groups": lax.rem(g + j, n_g)})

    def along_s(d, e, j, owner):
        b = lax.rem(a + n_a - d, n_a)
        q = lax.rem(g + n_g - e, n_g) * n_s + owner
        return parts(b, q, pc_sem, (d * n_g + e) * n_s + j, {"seq": lax.rem(s + j, n_s)})

    near_first = sorted(range(1, n_a), key=lambda d: (min(d, n_a - d), d))
    for d in near_first:
        for copy in along_a(d, a):
            copy.start()
    for d in near_first:
        send_u(d, a).start()
    for i in range(steps):
        load_x(i).start()

    def send_w(j, k, owner):
        at = at_rows(lax.rem(t + k, n_t), cols)
        return remote(
            w_hbm.at[:, at], w_v.at[at_rows(owner, w_rows), at],
            w_sem.at[0, j * n_t + k], w_sem.at[1, j * n_t + k], {"seq": lax.rem(s + j, n_s)},
        )

    order = list(range(1, n_t)) + [0]
    for k in order:
        for j in range(1, n_s):
            send_w(j, k, s).start()

    load_w.wait()

    def own_rows(i, _):
        load_x(i).wait()
        for k in range(n_t):
            base_part[k, at_rows(i)] = jnp.dot(
                x_v[at_rows(i), own_w], w_v[own_w, at_rows(lax.rem(t + k, n_t), cols)],
                preferred_element_type=F32,
            )
        return 0

    lax.fori_loop(0, steps, own_rows, 0)

    def other_rows(i, k):
        total = base_part[k, at_rows(i)]
        for j in range(1, n_s):
            at = at_rows(lax.rem(s + j, n_s), w_rows)
            total = total + jnp.dot(
                x_v[at_rows(i), at], w_v[at, at_rows(lax.rem(t + k, n_t), cols)],
                preferred_element_type=F32,
            )
        return total

    def send_base(j, i):
        k = (j - 1) * steps + i
        device = {"tensor": lax.rem(t + j, n_t)}
        return (
            remote(
                base_send.at[j - 1, at_rows(i)], base_recv.at[j - 1, at_rows(i)],
                base_sem.at[0, k], base_sem.at[1, k], device,
            ),
            remote(
                step_send.at[k], step_recv.at[k], step_sem.at[0, k], step_sem.at[1, k], device
            ),
        )

    for k in range(1, n_t):
        for j in range(1, n_s):
            send_w(j, k, lax.rem(s + n_s - j, n_s)).wait_recv()

        def other_columns(i, _):
            code, step = coded(other_rows(i, k))
            base_send[k - 1, at_rows(i)] = code
            step_send[(k - 1) * steps + i] = jnp.broadcast_to(step, step_send.shape[1:])
            for copy in send_base(k, i):
                copy.start()
            return 0

        lax.fori_loop(0, steps, other_columns, 0)

    def pass_on(d):
        for copy in along_a(d, lax.rem(a + n_a - d, n_a)):
            copy.wait_recv()
        for j in range(1, n_g):
            for copy in along_g(d, j, g):
                copy.start()
        for j in range(1, n_s):
            for copy in along_s(d, 0, j, s):
                copy.start()

    early = len(near_first) * 2 // 3
    for d in near_first[:early]:
        pass_on(d)

    for j in range(1, n_s):
        send_w(j, 0, lax.rem(s + n_s - j, n_s)).wait_recv()

    def own_columns(i, _):
        base_own[at_rows(i)] = other_rows(i, 0)
        return 0

    lax.fori_loop(0, steps, own_columns, 0)

    for d in near_first[early:]:
        pass_on(d)

    def reduce_part(q, fresh):
        at = at_rows(q, span)
        turned_v[...] = d_v[:, at].T

        def some(i, _):
            more = jnp.dot(x_v[at_rows(i), at], turned_v[...], preferred_element_type=F32)
            reduced_v[at_rows(i)] = more if fresh else reduced_v[at_rows(i)] + more
            return 0

        lax.fori_loop(0, steps, some, 0)

    reduce_part(g * n_s + s, True)
    for d in near_first:
        for j in range(1, n_g):
            for copy in along_g(d, j, lax.rem(g + n_g - j, n_g)):
                copy.wait_recv()
            for k in range(1, n_s):
                for copy in along_s(d, j, k, s):
                    copy.start()
    for e in range(n_g):
        at_g = lax.rem(g + n_g - e, n_g) * n_s
        if e:
            reduce_part(at_g + s, False)
        for k in range(1, n_s):
            owner = lax.rem(s + n_s - k, n_s)
            for d in near_first:
                for copy in along_s(d, e, k, owner):
                    copy.wait_recv()
            reduce_part(at_g + owner, False)

    short = chunk // 2

    def send_z(j, i):
        k = (j - 1) * steps + i
        device = {"tensor": lax.rem(t + j, n_t)}
        return (
            remote(
                z_send.at[at_rows(i, short)], z_recv.at[j - 1, at_rows(i, short)],
                z_sem.at[0, k], z_sem.at[1, k], device,
            ),
            remote(
                z_step_send.at[i], z_step_recv.at[k], z_step_sem.at[0, k], z_step_sem.at[1, k], device
            ),
        )

    def low_rank(i, _):
        index = index_v[at_rows(i)]
        partial = reduced_v[at_rows(i)]
        lane = lax.broadcasted_iota(jnp.int32, (chunk, 2 * rank), 1)
        is_right = (lane >= rank).astype(jnp.int32)
        total = jnp.zeros((chunk, 2 * rank), F32)
        for pair in range(n_a // 2):
            at = slice(2 * rank * pair, 2 * rank * (pair + 1))
            total += jnp.where(index == 2 * pair + is_right, partial[:, at], 0.0)
        total = total + pltpu.roll(total, rank, 1)
        total = jnp.where(lane[:short] < rank, total[:short], total[short:])
        z_own[at_rows(i, short)] = total
        code, step = coded(total)
        z_send[at_rows(i, short)] = code
        z_step_send[i] = jnp.broadcast_to(step, z_step_send.shape[1:])
        for j in range(1, n_t):
            for copy in send_z(j, i):
                copy.start()
        return 0

    lax.fori_loop(0, steps, low_rank, 0)

    for d in near_first:
        send_u(d, lax.rem(a + n_a - d, n_a)).wait_recv()

    def store_out(i):
        return pltpu.make_async_copy(o_v.at[at_rows(i)], o_hbm.at[at_rows(i)], out_sem.at[i])

    def finish(i, _):
        z = z_own[at_rows(i, short)]
        total = base_own[at_rows(i)]
        for j in range(1, n_t):
            for copy in send_base(j, i):
                copy.wait_recv()
            total = total + decoded(
                base_recv[j - 1, at_rows(i)], step_recv[(j - 1) * steps + i][:1]
            )
        for j in range(1, n_t):
            for copy in send_z(j, i):
                copy.wait_recv()
            z = z + decoded(z_recv[j - 1, at_rows(i, short)], z_step_recv[(j - 1) * steps + i][:1])
        turned = pltpu.roll(z, rank, 1)
        left = lax.broadcasted_iota(jnp.int32, (short, 2 * rank), 1) < rank
        both = jnp.concatenate([jnp.where(left, z, turned), jnp.where(left, turned, z)], axis=0)
        lane = lax.broadcasted_iota(jnp.int32, (chunk, 2 * rank), 1)
        is_right = (lane >= rank).astype(jnp.int32)
        index = index_v[at_rows(i)]
        spread = jnp.concatenate(
            [jnp.where(index == 2 * pair + is_right, both, 0.0) for pair in range(n_a // 2)], axis=1
        )
        high = spread.astype(BF16)
        low = (spread - high.astype(F32)).astype(BF16)
        total = total + jnp.dot(high, u_v[...], preferred_element_type=F32)
        total = total + jnp.dot(low, u_v[...], preferred_element_type=F32)
        o_v[at_rows(i)] = total.astype(BF16)
        store_out(i).start()
        return 0

    lax.fori_loop(0, steps, finish, 0)

    for d in near_first:
        send_u(d, a).wait_send()
    for k in order:
        for j in range(1, n_s):
            send_w(j, k, s).wait_send()
    for d in range(1, n_a):
        for copy in along_a(d, a):
            copy.wait_send()
        for j in range(1, n_g):
            for copy in along_g(d, j, g):
                copy.wait_send()
        for e in range(n_g):
            for k in range(1, n_s):
                for copy in along_s(d, e, k, s):
                    copy.wait_send()
    for i in range(steps):
        for j in range(1, n_t):
            for copy in send_base(j, i):
                copy.wait_send()
            for copy in send_z(j, i):
                copy.wait_send()
        store_out(i).wait()


def local(sizes, tokens, token_adapter_index, base_key_weight, lowrank_down_weight, lowrank_up_weight):
    n_g, n_a, n_t, n_s = sizes
    micro, tok_rows, width = tokens.shape
    rows = micro * tok_rows
    key_cols = base_key_weight.shape[1]
    cols = key_cols // n_t
    rank = lowrank_down_weight.shape[2]
    chunk = rows // 2
    steps = rows // chunk
    any_space = pl.BlockSpec(memory_space=pl.ANY)
    dma = pltpu.SemaphoreType.DMA
    out = pl.pallas_call(
        functools.partial(kernel, sizes, chunk),
        out_shape=jax.ShapeDtypeStruct((rows, cols), BF16),
        in_specs=[pl.BlockSpec(memory_space=pltpu.VMEM)] + [any_space] * 4,
        out_specs=any_space,
        scratch_shapes=[
            pltpu.VMEM((rows, 2 * rank), jnp.int32),
            pltpu.VMEM((rows, width), BF16),
            pltpu.VMEM((width, key_cols), BF16),
            pltpu.VMEM((n_a * rank, width), BF16),
            pltpu.VMEM((width // (n_g * n_s), n_a * rank), BF16),
            pltpu.VMEM((rows, n_a * rank), F32),
            pltpu.VMEM((n_a * rank, cols), BF16),
            pltpu.VMEM((n_t, rows, cols), F32),
            pltpu.VMEM((n_t - 1, rows, cols), jnp.int16),
            pltpu.VMEM((n_t - 1, rows, cols), jnp.int16),
            pltpu.VMEM(((n_t - 1) * steps, 8, cols), F32),
            pltpu.VMEM(((n_t - 1) * steps, 8, cols), F32),
            pltpu.VMEM((rows, cols), F32),
            pltpu.VMEM((rows // 2, 2 * rank), F32),
            pltpu.VMEM((rows // 2, 2 * rank), jnp.int16),
            pltpu.VMEM((n_t - 1, rows // 2, 2 * rank), jnp.int16),
            pltpu.VMEM((steps, 8, 2 * rank), F32),
            pltpu.VMEM(((n_t - 1) * steps, 8, 2 * rank), F32),
            pltpu.VMEM((rows, cols), BF16),
            dma((steps,)),
            dma((3,)),
            dma((steps,)),
            dma((2, n_s * n_t)),
            dma((2, n_a)),
            dma((2, n_a * n_g)),
            dma((2, n_a * n_g * n_s)),
            dma((2, n_a)),
            dma((2, (n_t - 1) * steps)),
            dma((2, (n_t - 1) * steps)),
            dma((2, (n_t - 1) * steps)),
            dma((2, (n_t - 1) * steps)),
        ],
        compiler_params=pltpu.CompilerParams(
            collective_id=0, has_side_effects=True, vmem_limit_bytes=56 * 1024 * 1024
        ),
    )(
        token_adapter_index.reshape(1, rows),
        tokens.reshape(rows, width),
        base_key_weight,
        jnp.swapaxes(lowrank_down_weight, 1, 2),
        lowrank_up_weight,
    )
    return out.reshape(micro, tok_rows, cols)


def solution(mesh):
    sizes = tuple(mesh.shape[name] for name in ("groups", "adapter", "tensor", "seq"))
    placed = (
        P(None, ("groups", "adapter", "seq"), "tensor"),
        P(None, ("groups", "adapter", "seq"), None),
        P(("tensor", "seq"), None),
        P("adapter", "tensor", None),
        P("adapter", None, None),
    )
    return jax.shard_map(
        functools.partial(local, sizes),
        mesh=mesh,
        in_specs=placed,
        out_specs=P(None, ("groups", "adapter", "seq"), "tensor"),
        check_vma=False,
    )
```

```python
import functools

import jax
import jax.numpy as jnp
from jax import lax
from jax.experimental import pallas as pl
from jax.experimental.pallas import tpu as pltpu
from jax.sharding import PartitionSpec as P

F32 = jnp.float32
BF16 = jnp.bfloat16
MESH = pl.DeviceIdType.MESH


def remote(src, dst, send, recv, device):
    return pltpu.make_async_remote_copy(
        src_ref=src, dst_ref=dst, send_sem=send, recv_sem=recv, device_id=device, device_id_type=MESH
    )


def coded(value):
    top = jnp.maximum(jnp.max(jnp.abs(value), axis=0, keepdims=True), 1e-30)
    return jnp.round(value * (32767.0 / top)).astype(jnp.int32).astype(jnp.int16), top * (1.0 / 32767.0)


def decoded(code, step):
    return code.astype(jnp.int32).astype(F32) * step


def kernel(
    sizes, chunk,
    idx_ref, x_hbm, w_hbm, d_hbm, u_hbm, o_hbm,
    index_v, x_v, w_v, d_v, reduced_v, u_v,
    base_part, base_send, base_recv, step_send, step_recv, base_own, z_own, z_send, z_recv, z_step_send, z_step_recv, o_v,
    x_sem, load_sem, out_sem, w_sem, pz_sem, py_sem, pc_sem, uz_sem, base_sem, step_sem, z_sem, z_step_sem,
):
    n_g, n_a, n_t, n_s = sizes
    g, a, t, s = [lax.axis_index(name) for name in ("groups", "adapter", "tensor", "seq")]
    rows, width = x_v.shape
    rank = d_hbm.shape[1]
    n_q = n_g * n_s
    span = width // n_q
    cols = o_v.shape[1]
    steps = rows // chunk
    w_rows = w_hbm.shape[0]

    def at_rows(i, size=chunk):
        return pl.ds(pl.multiple_of(i * size, size), size)

    def load_x(i):
        return pltpu.make_async_copy(x_hbm.at[at_rows(i)], x_v.at[at_rows(i)], x_sem.at[i])

    own_w = at_rows(s, w_rows)
    own_cols = at_rows(t, cols)
    own_rank = at_rows(a, rank)
    load_d = pltpu.make_async_copy(d_hbm.at[0], d_v.at[own_rank], load_sem.at[0])
    load_u = pltpu.make_async_copy(u_hbm.at[0, :, own_cols], u_v.at[own_rank], load_sem.at[1])
    load_w = pltpu.make_async_copy(w_hbm, w_v.at[own_w], load_sem.at[2])
    load_d.start()
    load_u.start()
    load_w.start()

    barrier = pltpu.get_barrier_semaphore()
    peers = [("groups", g, n_g), ("adapter", a, n_a), ("tensor", t, n_t), ("seq", s, n_s)]
    for name, at, size in peers:
        for j in range(1, size):
            pl.semaphore_signal(
                barrier, inc=1, device_id={name: lax.rem(at + j, size)}, device_id_type=MESH
            )

    for i in range(rows // 128):
        line = jnp.broadcast_to(idx_ref[:, i * 128 : (i + 1) * 128], (128, 128))
        index_v[i * 128 : (i + 1) * 128] = line.T

    load_d.wait()
    load_u.wait()
    pl.semaphore_wait(barrier, sum(size - 1 for _, _, size in peers))

    def parts(b, q, sems_p, k, device):
        p_at = d_v.at[at_rows(b, rank), at_rows(q, span)]
        return (remote(p_at, p_at, sems_p.at[0, k], sems_p.at[1, k], device),)

    def send_u(d, source):
        at = u_v.at[at_rows(source, rank)]
        return remote(at, at, uz_sem.at[0, d], uz_sem.at[1, d], {"adapter": lax.rem(a + d, n_a)})

    def along_a(d, source):
        return parts(source, g * n_s + s, pz_sem, d, {"adapter": lax.rem(a + d, n_a)})

    def along_g(d, j, owner):
        b = lax.rem(a + n_a - d, n_a)
        return parts(b, owner * n_s + s, py_sem, d * n_g + j, {"groups": lax.rem(g + j, n_g)})

    def along_s(d, e, j, owner):
        b = lax.rem(a + n_a - d, n_a)
        q = lax.rem(g + n_g - e, n_g) * n_s + owner
        return parts(b, q, pc_sem, (d * n_g + e) * n_s + j, {"seq": lax.rem(s + j, n_s)})

    near_first = sorted(range(1, n_a), key=lambda d: (min(d, n_a - d), d))
    for d in near_first:
        for copy in along_a(d, a):
            copy.start()
    for d in near_first:
        send_u(d, a).start()
    for i in range(steps):
        load_x(i).start()

    def send_w(j, k, owner):
        at = at_rows(lax.rem(t + k, n_t), cols)
        return remote(
            w_hbm.at[:, at], w_v.at[at_rows(owner, w_rows), at],
            w_sem.at[0, j * n_t + k], w_sem.at[1, j * n_t + k], {"seq": lax.rem(s + j, n_s)},
        )

    order = list(range(1, n_t)) + [0]
    for k in order:
        for j in range(1, n_s):
            send_w(j, k, s).start()

    load_w.wait()

    def own_rows(i, _):
        load_x(i).wait()
        for k in range(n_t):
            base_part[k, at_rows(i)] = jnp.dot(
                x_v[at_rows(i), own_w], w_v[own_w, at_rows(lax.rem(t + k, n_t), cols)],
                preferred_element_type=F32,
            )
        return 0

    lax.fori_loop(0, steps, own_rows, 0)

    def other_rows(i, k):
        total = base_part[k, at_rows(i)]
        for j in range(1, n_s):
            at = at_rows(lax.rem(s + j, n_s), w_rows)
            total = total + jnp.dot(
                x_v[at_rows(i), at], w_v[at, at_rows(lax.rem(t + k, n_t), cols)],
                preferred_element_type=F32,
            )
        return total

    def send_base(j, i):
        k = (j - 1) * steps + i
        device = {"tensor": lax.rem(t + j, n_t)}
        return (
            remote(
                base_send.at[j - 1, at_rows(i)], base_recv.at[j - 1, at_rows(i)],
                base_sem.at[0, k], base_sem.at[1, k], device,
            ),
            remote(
                step_send.at[k], step_recv.at[k], step_sem.at[0, k], step_sem.at[1, k], device
            ),
        )

    for k in range(1, n_t):
        for j in range(1, n_s):
            send_w(j, k, lax.rem(s + n_s - j, n_s)).wait_recv()

        def other_columns(i, _):
            code, step = coded(other_rows(i, k))
            base_send[k - 1, at_rows(i)] = code
            step_send[(k - 1) * steps + i] = jnp.broadcast_to(step, step_send.shape[1:])
            for copy in send_base(k, i):
                copy.start()
            return 0

        lax.fori_loop(0, steps, other_columns, 0)

    def pass_on(d):
        for copy in along_a(d, lax.rem(a + n_a - d, n_a)):
            copy.wait_recv()
        for j in range(1, n_g):
            for copy in along_g(d, j, g):
                copy.start()
        for j in range(1, n_s):
            for copy in along_s(d, 0, j, s):
                copy.start()

    early = len(near_first) * 2 // 3
    for d in near_first[:early]:
        pass_on(d)

    for j in range(1, n_s):
        send_w(j, 0, lax.rem(s + n_s - j, n_s)).wait_recv()

    def own_columns(i, _):
        base_own[at_rows(i)] = other_rows(i, 0)
        return 0

    lax.fori_loop(0, steps, own_columns, 0)

    for d in near_first[early:]:
        pass_on(d)

    short = chunk // 2

    def send_z(j, i):
        k = (j - 1) * steps + i
        device = {"tensor": lax.rem(t + j, n_t)}
        return (
            remote(
                z_send.at[at_rows(i, short)], z_recv.at[j - 1, at_rows(i, short)],
                z_sem.at[0, k], z_sem.at[1, k], device,
            ),
            remote(
                z_step_send.at[i], z_step_recv.at[k], z_step_sem.at[0, k], z_step_sem.at[1, k], device
            ),
        )

    def low_rank(i, _):
        index = index_v[at_rows(i)]
        partial = reduced_v[at_rows(i)]
        lane = lax.broadcasted_iota(jnp.int32, (chunk, 2 * rank), 1)
        is_right = (lane >= rank).astype(jnp.int32)
        total = jnp.zeros((chunk, 2 * rank), F32)
        for pair in range(n_a // 2):
            at = slice(2 * rank * pair, 2 * rank * (pair + 1))
            total += jnp.where(index == 2 * pair + is_right, partial[:, at], 0.0)
        total = total + pltpu.roll(total, rank, 1)
        total = jnp.where(lane[:short] < rank, total[:short], total[short:])
        z_own[at_rows(i, short)] = total
        code, step = coded(total)
        z_send[at_rows(i, short)] = code
        z_step_send[i] = jnp.broadcast_to(step, z_step_send.shape[1:])
        for j in range(1, n_t):
            for copy in send_z(j, i):
                copy.start()
        return 0

    def reduce_part(q, fresh, last=False):
        at = at_rows(q, span)

        def some(i, _):
            more = lax.dot_general(
                x_v[at_rows(i), at], d_v[:, at], (((1,), (1,)), ((), ())), preferred_element_type=F32
            )
            reduced_v[at_rows(i)] = more if fresh else reduced_v[at_rows(i)] + more
            if last:
                low_rank(i, 0)
            return 0

        lax.fori_loop(0, steps, some, 0)

    reduce_part(g * n_s + s, True)
    for d in near_first:
        for j in range(1, n_g):
            for copy in along_g(d, j, lax.rem(g + n_g - j, n_g)):
                copy.wait_recv()
            for k in range(1, n_s):
                for copy in along_s(d, j, k, s):
                    copy.start()
    for e in range(n_g):
        at_g = lax.rem(g + n_g - e, n_g) * n_s
        if e:
            reduce_part(at_g + s, False)
        for k in range(1, n_s):
            owner = lax.rem(s + n_s - k, n_s)
            for d in near_first:
                for copy in along_s(d, e, k, owner):
                    copy.wait_recv()
            reduce_part(at_g + owner, False, e == n_g - 1 and k == n_s - 1)


    for d in near_first:
        send_u(d, lax.rem(a + n_a - d, n_a)).wait_recv()

    def store_out(i):
        return pltpu.make_async_copy(o_v.at[at_rows(i)], o_hbm.at[at_rows(i)], out_sem.at[i])

    def finish(i, _):
        z = z_own[at_rows(i, short)]
        total = base_own[at_rows(i)]
        for j in range(1, n_t):
            for copy in send_base(j, i):
                copy.wait_recv()
            total = total + decoded(
                base_recv[j - 1, at_rows(i)], step_recv[(j - 1) * steps + i][:1]
            )
        for j in range(1, n_t):
            for copy in send_z(j, i):
                copy.wait_recv()
            z = z + decoded(z_recv[j - 1, at_rows(i, short)], z_step_recv[(j - 1) * steps + i][:1])
        turned = pltpu.roll(z, rank, 1)
        left = lax.broadcasted_iota(jnp.int32, (short, 2 * rank), 1) < rank
        both = jnp.concatenate([jnp.where(left, z, turned), jnp.where(left, turned, z)], axis=0)
        lane = lax.broadcasted_iota(jnp.int32, (chunk, 2 * rank), 1)
        is_right = (lane >= rank).astype(jnp.int32)
        index = index_v[at_rows(i)]
        spread = jnp.concatenate(
            [jnp.where(index == 2 * pair + is_right, both, 0.0) for pair in range(n_a // 2)], axis=1
        )
        high = spread.astype(BF16)
        low = (spread - high.astype(F32)).astype(BF16)
        total = total + jnp.dot(high, u_v[...], preferred_element_type=F32)
        total = total + jnp.dot(low, u_v[...], preferred_element_type=F32)
        o_v[at_rows(i)] = total.astype(BF16)
        store_out(i).start()
        return 0

    lax.fori_loop(0, steps, finish, 0)

    for d in near_first:
        send_u(d, a).wait_send()
    for k in order:
        for j in range(1, n_s):
            send_w(j, k, s).wait_send()
    for d in range(1, n_a):
        for copy in along_a(d, a):
            copy.wait_send()
        for j in range(1, n_g):
            for copy in along_g(d, j, g):
                copy.wait_send()
        for e in range(n_g):
            for k in range(1, n_s):
                for copy in along_s(d, e, k, s):
                    copy.wait_send()
    for i in range(steps):
        for j in range(1, n_t):
            for copy in send_base(j, i):
                copy.wait_send()
            for copy in send_z(j, i):
                copy.wait_send()
        store_out(i).wait()


def local(sizes, tokens, token_adapter_index, base_key_weight, lowrank_down_weight, lowrank_up_weight):
    n_g, n_a, n_t, n_s = sizes
    micro, tok_rows, width = tokens.shape
    rows = micro * tok_rows
    key_cols = base_key_weight.shape[1]
    cols = key_cols // n_t
    rank = lowrank_down_weight.shape[2]
    chunk = rows // 2
    steps = rows // chunk
    any_space = pl.BlockSpec(memory_space=pl.ANY)
    dma = pltpu.SemaphoreType.DMA
    out = pl.pallas_call(
        functools.partial(kernel, sizes, chunk),
        out_shape=jax.ShapeDtypeStruct((rows, cols), BF16),
        in_specs=[pl.BlockSpec(memory_space=pltpu.VMEM)] + [any_space] * 4,
        out_specs=any_space,
        scratch_shapes=[
            pltpu.VMEM((rows, 2 * rank), jnp.int32),
            pltpu.VMEM((rows, width), BF16),
            pltpu.VMEM((width, key_cols), BF16),
            pltpu.VMEM((n_a * rank, width), BF16),
            pltpu.VMEM((rows, n_a * rank), F32),
            pltpu.VMEM((n_a * rank, cols), BF16),
            pltpu.VMEM((n_t, rows, cols), F32),
            pltpu.VMEM((n_t - 1, rows, cols), jnp.int16),
            pltpu.VMEM((n_t - 1, rows, cols), jnp.int16),
            pltpu.VMEM(((n_t - 1) * steps, 8, cols), F32),
            pltpu.VMEM(((n_t - 1) * steps, 8, cols), F32),
            pltpu.VMEM((rows, cols), F32),
            pltpu.VMEM((rows // 2, 2 * rank), F32),
            pltpu.VMEM((rows // 2, 2 * rank), jnp.int16),
            pltpu.VMEM((n_t - 1, rows // 2, 2 * rank), jnp.int16),
            pltpu.VMEM((steps, 8, 2 * rank), F32),
            pltpu.VMEM(((n_t - 1) * steps, 8, 2 * rank), F32),
            pltpu.VMEM((rows, cols), BF16),
            dma((steps,)),
            dma((3,)),
            dma((steps,)),
            dma((2, n_s * n_t)),
            dma((2, n_a)),
            dma((2, n_a * n_g)),
            dma((2, n_a * n_g * n_s)),
            dma((2, n_a)),
            dma((2, (n_t - 1) * steps)),
            dma((2, (n_t - 1) * steps)),
            dma((2, (n_t - 1) * steps)),
            dma((2, (n_t - 1) * steps)),
        ],
        compiler_params=pltpu.CompilerParams(
            collective_id=0, has_side_effects=True, vmem_limit_bytes=56 * 1024 * 1024
        ),
    )(
        token_adapter_index.reshape(1, rows),
        tokens.reshape(rows, width),
        base_key_weight,
        jnp.swapaxes(lowrank_down_weight, 1, 2),
        lowrank_up_weight,
    )
    return out.reshape(micro, tok_rows, cols)


def solution(mesh):
    sizes = tuple(mesh.shape[name] for name in ("groups", "adapter", "tensor", "seq"))
    placed = (
        P(None, ("groups", "adapter", "seq"), "tensor"),
        P(None, ("groups", "adapter", "seq"), None),
        P(("tensor", "seq"), None),
        P("adapter", "tensor", None),
        P("adapter", None, None),
    )
    return jax.shard_map(
        functools.partial(local, sizes),
        mesh=mesh,
        in_specs=placed,
        out_specs=P(None, ("groups", "adapter", "seq"), "tensor"),
        check_vma=False,
    )
```

```python
import functools

import jax
import jax.numpy as jnp
from jax import lax
from jax.experimental import pallas as pl
from jax.experimental.pallas import tpu as pltpu
from jax.sharding import PartitionSpec as P

F32 = jnp.float32
BF16 = jnp.bfloat16
MESH = pl.DeviceIdType.MESH


def remote(src, dst, send, recv, device):
    return pltpu.make_async_remote_copy(
        src_ref=src, dst_ref=dst, send_sem=send, recv_sem=recv, device_id=device, device_id_type=MESH
    )


def coded(value):
    top = jnp.maximum(jnp.max(jnp.abs(value), axis=0, keepdims=True), 1e-30)
    return jnp.round(value * (32767.0 / top)).astype(jnp.int32).astype(jnp.int16), top * (1.0 / 32767.0)


def decoded(code, step):
    return code.astype(jnp.int32).astype(F32) * step


def kernel(
    sizes, chunk,
    idx_ref, x_hbm, w_hbm, d_hbm, u_hbm, o_hbm,
    index_v, x_v, w_v, d_v, reduced_v, u_v,
    base_part, base_send, base_recv, step_send, step_recv, base_own, z_own, z_send, z_recv, z_step_send, z_step_recv, o_v,
    x_sem, load_sem, out_sem, w_sem, pz_sem, py_sem, pc_sem, uz_sem, base_sem, step_sem, z_sem, z_step_sem,
):
    n_g, n_a, n_t, n_s = sizes
    g, a, t, s = [lax.axis_index(name) for name in ("groups", "adapter", "tensor", "seq")]
    rows, width = x_v.shape
    rank = d_hbm.shape[1]
    n_q = n_g * n_s
    span = width // n_q
    cols = o_v.shape[1]
    steps = rows // chunk
    w_rows = w_hbm.shape[0]

    def at_rows(i, size=chunk):
        return pl.ds(pl.multiple_of(i * size, size), size)

    def load_x(i):
        return pltpu.make_async_copy(x_hbm.at[at_rows(i)], x_v.at[at_rows(i)], x_sem.at[i])

    own_w = at_rows(s, w_rows)
    own_cols = at_rows(t, cols)
    own_rank = at_rows(a, rank)
    load_d = pltpu.make_async_copy(d_hbm.at[0], d_v.at[own_rank], load_sem.at[0])
    load_u = pltpu.make_async_copy(u_hbm.at[0, :, own_cols], u_v.at[own_rank], load_sem.at[1])
    load_w = pltpu.make_async_copy(w_hbm, w_v.at[own_w], load_sem.at[2])
    load_d.start()
    load_u.start()
    load_w.start()

    barrier = pltpu.get_barrier_semaphore()
    peers = [("groups", g, n_g), ("adapter", a, n_a), ("tensor", t, n_t), ("seq", s, n_s)]
    for name, at, size in peers:
        for j in range(1, size):
            pl.semaphore_signal(
                barrier, inc=1, device_id={name: lax.rem(at + j, size)}, device_id_type=MESH
            )

    for i in range(rows // 128):
        line = jnp.broadcast_to(idx_ref[:, i * 128 : (i + 1) * 128], (128, 128))
        index_v[i * 128 : (i + 1) * 128] = line.T

    load_d.wait()
    load_u.wait()
    pl.semaphore_wait(barrier, sum(size - 1 for _, _, size in peers))

    def parts(b, q, sems_p, k, device):
        p_at = d_v.at[at_rows(b, rank), at_rows(q, span)]
        return (remote(p_at, p_at, sems_p.at[0, k], sems_p.at[1, k], device),)

    def send_u(d, source):
        at = u_v.at[at_rows(source, rank)]
        return remote(at, at, uz_sem.at[0, d], uz_sem.at[1, d], {"adapter": lax.rem(a + d, n_a)})

    def along_a(d, source):
        return parts(source, g * n_s + s, pz_sem, d, {"adapter": lax.rem(a + d, n_a)})

    def along_g(d, j, owner):
        b = lax.rem(a + n_a - d, n_a)
        return parts(b, owner * n_s + s, py_sem, d * n_g + j, {"groups": lax.rem(g + j, n_g)})

    def along_s(d, e, j, owner):
        b = lax.rem(a + n_a - d, n_a)
        q = lax.rem(g + n_g - e, n_g) * n_s + owner
        return parts(b, q, pc_sem, (d * n_g + e) * n_s + j, {"seq": lax.rem(s + j, n_s)})

    far_first = sorted(range(1, n_a), key=lambda d: (-min(d, n_a - d), d))
    for d in far_first:
        for copy in along_a(d, a):
            copy.start()
    for d in far_first:
        send_u(d, a).start()
    for i in range(steps):
        load_x(i).start()

    def send_w(j, k, owner):
        at = at_rows(lax.rem(t + k, n_t), cols)
        return remote(
            w_hbm.at[:, at], w_v.at[at_rows(owner, w_rows), at],
            w_sem.at[0, j * n_t + k], w_sem.at[1, j * n_t + k], {"seq": lax.rem(s + j, n_s)},
        )

    order = list(range(1, n_t)) + [0]
    for k in order:
        for j in range(1, n_s):
            send_w(j, k, s).start()

    load_w.wait()

    def own_rows(i, _):
        load_x(i).wait()
        for k in range(n_t):
            base_part[k, at_rows(i)] = jnp.dot(
                x_v[at_rows(i), own_w], w_v[own_w, at_rows(lax.rem(t + k, n_t), cols)],
                preferred_element_type=F32,
            )
        return 0

    lax.fori_loop(0, steps, own_rows, 0)

    def other_rows(i, k):
        total = base_part[k, at_rows(i)]
        for j in range(1, n_s):
            at = at_rows(lax.rem(s + j, n_s), w_rows)
            total = total + jnp.dot(
                x_v[at_rows(i), at], w_v[at, at_rows(lax.rem(t + k, n_t), cols)],
                preferred_element_type=F32,
            )
        return total

    def send_base(j, i):
        k = (j - 1) * steps + i
        device = {"tensor": lax.rem(t + j, n_t)}
        return (
            remote(
                base_send.at[j - 1, at_rows(i)], base_recv.at[j - 1, at_rows(i)],
                base_sem.at[0, k], base_sem.at[1, k], device,
            ),
            remote(
                step_send.at[k], step_recv.at[k], step_sem.at[0, k], step_sem.at[1, k], device
            ),
        )

    for k in range(1, n_t):
        for j in range(1, n_s):
            send_w(j, k, lax.rem(s + n_s - j, n_s)).wait_recv()

        def other_columns(i, _):
            code, step = coded(other_rows(i, k))
            base_send[k - 1, at_rows(i)] = code
            step_send[(k - 1) * steps + i] = jnp.broadcast_to(step, step_send.shape[1:])
            for copy in send_base(k, i):
                copy.start()
            return 0

        lax.fori_loop(0, steps, other_columns, 0)

    def pass_on(d):
        for copy in along_a(d, lax.rem(a + n_a - d, n_a)):
            copy.wait_recv()
        for j in range(1, n_g):
            for copy in along_g(d, j, g):
                copy.start()
        for j in range(1, n_s):
            for copy in along_s(d, 0, j, s):
                copy.start()

    early = len(far_first) * 2 // 3
    for d in far_first[:early]:
        pass_on(d)

    for j in range(1, n_s):
        send_w(j, 0, lax.rem(s + n_s - j, n_s)).wait_recv()

    def own_columns(i, _):
        base_own[at_rows(i)] = other_rows(i, 0)
        return 0

    lax.fori_loop(0, steps, own_columns, 0)

    for d in far_first[early:]:
        pass_on(d)

    short = chunk // 2

    def send_z(j, i):
        k = (j - 1) * steps + i
        device = {"tensor": lax.rem(t + j, n_t)}
        return (
            remote(
                z_send.at[at_rows(i, short)], z_recv.at[j - 1, at_rows(i, short)],
                z_sem.at[0, k], z_sem.at[1, k], device,
            ),
            remote(
                z_step_send.at[i], z_step_recv.at[k], z_step_sem.at[0, k], z_step_sem.at[1, k], device
            ),
        )

    def low_rank(i, _):
        index = index_v[at_rows(i)]
        partial = reduced_v[at_rows(i)]
        lane = lax.broadcasted_iota(jnp.int32, (chunk, 2 * rank), 1)
        is_right = (lane >= rank).astype(jnp.int32)
        total = jnp.zeros((chunk, 2 * rank), F32)
        for pair in range(n_a // 2):
            at = slice(2 * rank * pair, 2 * rank * (pair + 1))
            total += jnp.where(index == 2 * pair + is_right, partial[:, at], 0.0)
        total = total + pltpu.roll(total, rank, 1)
        total = jnp.where(lane[:short] < rank, total[:short], total[short:])
        z_own[at_rows(i, short)] = total
        code, step = coded(total)
        z_send[at_rows(i, short)] = code
        z_step_send[i] = jnp.broadcast_to(step, z_step_send.shape[1:])
        for j in range(1, n_t):
            for copy in send_z(j, i):
                copy.start()
        return 0

    def reduce_part(q, fresh, last=False):
        at = at_rows(q, span)

        def some(i, _):
            more = lax.dot_general(
                x_v[at_rows(i), at], d_v[:, at], (((1,), (1,)), ((), ())), preferred_element_type=F32
            )
            reduced_v[at_rows(i)] = more if fresh else reduced_v[at_rows(i)] + more
            if last:
                low_rank(i, 0)
            return 0

        lax.fori_loop(0, steps, some, 0)

    reduce_part(g * n_s + s, True)
    for d in far_first:
        for j in range(1, n_g):
            for copy in along_g(d, j, lax.rem(g + n_g - j, n_g)):
                copy.wait_recv()
            for k in range(1, n_s):
                for copy in along_s(d, j, k, s):
                    copy.start()
    for e in range(n_g):
        at_g = lax.rem(g + n_g - e, n_g) * n_s
        if e:
            reduce_part(at_g + s, False)
        for k in range(1, n_s):
            owner = lax.rem(s + n_s - k, n_s)
            for d in far_first:
                for copy in along_s(d, e, k, owner):
                    copy.wait_recv()
            reduce_part(at_g + owner, False, e == n_g - 1 and k == n_s - 1)


    for d in far_first:
        send_u(d, lax.rem(a + n_a - d, n_a)).wait_recv()

    def store_out(i):
        return pltpu.make_async_copy(o_v.at[at_rows(i)], o_hbm.at[at_rows(i)], out_sem.at[i])

    def finish(i, _):
        z = z_own[at_rows(i, short)]
        total = base_own[at_rows(i)]
        for j in range(1, n_t):
            for copy in send_base(j, i):
                copy.wait_recv()
            total = total + decoded(
                base_recv[j - 1, at_rows(i)], step_recv[(j - 1) * steps + i][:1]
            )
        for j in range(1, n_t):
            for copy in send_z(j, i):
                copy.wait_recv()
            z = z + decoded(z_recv[j - 1, at_rows(i, short)], z_step_recv[(j - 1) * steps + i][:1])
        turned = pltpu.roll(z, rank, 1)
        left = lax.broadcasted_iota(jnp.int32, (short, 2 * rank), 1) < rank
        both = jnp.concatenate([jnp.where(left, z, turned), jnp.where(left, turned, z)], axis=0)
        lane = lax.broadcasted_iota(jnp.int32, (chunk, 2 * rank), 1)
        is_right = (lane >= rank).astype(jnp.int32)
        index = index_v[at_rows(i)]
        spread = jnp.concatenate(
            [jnp.where(index == 2 * pair + is_right, both, 0.0) for pair in range(n_a // 2)], axis=1
        )
        high = spread.astype(BF16)
        low = (spread - high.astype(F32)).astype(BF16)
        total = total + jnp.dot(high, u_v[...], preferred_element_type=F32)
        total = total + jnp.dot(low, u_v[...], preferred_element_type=F32)
        o_v[at_rows(i)] = total.astype(BF16)
        store_out(i).start()
        return 0

    lax.fori_loop(0, steps, finish, 0)

    for d in far_first:
        send_u(d, a).wait_send()
    for k in order:
        for j in range(1, n_s):
            send_w(j, k, s).wait_send()
    for d in range(1, n_a):
        for copy in along_a(d, a):
            copy.wait_send()
        for j in range(1, n_g):
            for copy in along_g(d, j, g):
                copy.wait_send()
        for e in range(n_g):
            for k in range(1, n_s):
                for copy in along_s(d, e, k, s):
                    copy.wait_send()
    for i in range(steps):
        for j in range(1, n_t):
            for copy in send_base(j, i):
                copy.wait_send()
            for copy in send_z(j, i):
                copy.wait_send()
        store_out(i).wait()


def local(sizes, tokens, token_adapter_index, base_key_weight, lowrank_down_weight, lowrank_up_weight):
    n_g, n_a, n_t, n_s = sizes
    micro, tok_rows, width = tokens.shape
    rows = micro * tok_rows
    key_cols = base_key_weight.shape[1]
    cols = key_cols // n_t
    rank = lowrank_down_weight.shape[2]
    chunk = rows // 2
    steps = rows // chunk
    any_space = pl.BlockSpec(memory_space=pl.ANY)
    dma = pltpu.SemaphoreType.DMA
    out = pl.pallas_call(
        functools.partial(kernel, sizes, chunk),
        out_shape=jax.ShapeDtypeStruct((rows, cols), BF16),
        in_specs=[pl.BlockSpec(memory_space=pltpu.VMEM)] + [any_space] * 4,
        out_specs=any_space,
        scratch_shapes=[
            pltpu.VMEM((rows, 2 * rank), jnp.int32),
            pltpu.VMEM((rows, width), BF16),
            pltpu.VMEM((width, key_cols), BF16),
            pltpu.VMEM((n_a * rank, width), BF16),
            pltpu.VMEM((rows, n_a * rank), F32),
            pltpu.VMEM((n_a * rank, cols), BF16),
            pltpu.VMEM((n_t, rows, cols), F32),
            pltpu.VMEM((n_t - 1, rows, cols), jnp.int16),
            pltpu.VMEM((n_t - 1, rows, cols), jnp.int16),
            pltpu.VMEM(((n_t - 1) * steps, 8, cols), F32),
            pltpu.VMEM(((n_t - 1) * steps, 8, cols), F32),
            pltpu.VMEM((rows, cols), F32),
            pltpu.VMEM((rows // 2, 2 * rank), F32),
            pltpu.VMEM((rows // 2, 2 * rank), jnp.int16),
            pltpu.VMEM((n_t - 1, rows // 2, 2 * rank), jnp.int16),
            pltpu.VMEM((steps, 8, 2 * rank), F32),
            pltpu.VMEM(((n_t - 1) * steps, 8, 2 * rank), F32),
            pltpu.VMEM((rows, cols), BF16),
            dma((steps,)),
            dma((3,)),
            dma((steps,)),
            dma((2, n_s * n_t)),
            dma((2, n_a)),
            dma((2, n_a * n_g)),
            dma((2, n_a * n_g * n_s)),
            dma((2, n_a)),
            dma((2, (n_t - 1) * steps)),
            dma((2, (n_t - 1) * steps)),
            dma((2, (n_t - 1) * steps)),
            dma((2, (n_t - 1) * steps)),
        ],
        compiler_params=pltpu.CompilerParams(
            collective_id=0, has_side_effects=True, vmem_limit_bytes=56 * 1024 * 1024
        ),
    )(
        token_adapter_index.reshape(1, rows),
        tokens.reshape(rows, width),
        base_key_weight,
        jnp.swapaxes(lowrank_down_weight, 1, 2),
        lowrank_up_weight,
    )
    return out.reshape(micro, tok_rows, cols)


def solution(mesh):
    sizes = tuple(mesh.shape[name] for name in ("groups", "adapter", "tensor", "seq"))
    placed = (
        P(None, ("groups", "adapter", "seq"), "tensor"),
        P(None, ("groups", "adapter", "seq"), None),
        P(("tensor", "seq"), None),
        P("adapter", "tensor", None),
        P("adapter", None, None),
    )
    return jax.shard_map(
        functools.partial(local, sizes),
        mesh=mesh,
        in_specs=placed,
        out_specs=P(None, ("groups", "adapter", "seq"), "tensor"),
        check_vma=False,
    )
```
